256 devices in a mesh: shot: 64 (over x, y, z_lo, core), head: 4 (over z_hi).
Axes of the slice: x: 4, y: 4, z: 8 (z_hi: 4, z_lo: 2; z = z_hi * 2 + z_lo), core: 2. Of those that a mesh axis runs over, the one named last changes fastest.
Arguments:
- summary_states: bfloat16 [1024, 4096], P('shot', 'head'), may hold values from -6 to 6
- summary_queries: bfloat16 [1024, 4096], P('shot', 'head'), may hold values from -360 to 360
- summary_keys: bfloat16 [1024, 4096], P('shot', 'head'), may hold values from -6 to 6
- summary_values: bfloat16 [1024, 4096], P('shot', 'head'), may hold values from -6 to 6
- demo_keys: bfloat16 [128, 512, 4096], P('shot', None, 'head'), may hold values from -6 to 6
- demo_values: bfloat16 [128, 512, 4096], P('shot', None, 'head'), may hold values from -6 to 6
- demo_lengths: int32 [128], P('shot'), may hold values from 128 to 512
- out_weight: bfloat16 [4096, 4096], P('head', 'shot'), may hold values from -0.09375 to 0.09375
- norm_gain: float32 [4096], P('head'), may hold values from 0.5 to 1.5
- key_weight: bfloat16 [4096, 4096], P('shot', 'head'), may hold values from -0.09375 to 0.09375
- value_weight: bfloat16 [4096, 4096], P('shot', 'head'), may hold values from -0.09375 to 0.09375
- query_queries: bfloat16 [65536, 4096], P('shot', 'head'), may hold values from -360 to 360
- query_keys: bfloat16 [65536, 4096], P('shot', 'head'), may hold values from -6 to 6
- query_values: bfloat16 [65536, 4096], P('shot', 'head'), may hold values from -6 to 6
- query_offsets: int32 [512], P('shot'), may hold values from 0 to 128
Outputs:
- answer: bfloat16 [65536, 4096], P('shot', 'head')
The draws below stay inside these ranges and needn't reach their ends.
All inputs are finite; a program needn't handle non-finite values.
Results may differ from the reference program's by a relative error of at most 0.024.
Values may be sent and summed in bfloat16 or wider, within the bound.
No kernel may reach another device: no remote copies, remote signals or barrier semaphores. Data moves between devices by JAX's collectives and lax.ppermute only.
A program may use at most 128 MiB of HBM per device.

```python
import jax
import jax.numpy as jnp
from jax import lax

D = 4096
H = 32
HD = 128
SLOTS = 8
CACHE = 512
QLEN = 128
DEMOS = 128
NSUM = 1024
QTOKENS = 65536


def spread_rows(key, rows, cols, share, low, high):
    base = jax.random.truncated_normal(jax.random.fold_in(key, 1), -6.0, 6.0, (rows, cols), jnp.float32)
    picked = jax.random.uniform(jax.random.fold_in(key, 2), (rows, 1)) < share
    boost = jax.random.uniform(jax.random.fold_in(key, 3), (rows, 1), minval=low, maxval=high)
    return base * jnp.where(picked, boost, 1.0)


def draw_summary_queries(key, part):
    key = jax.random.fold_in(key, 11)
    values = spread_rows(key, NSUM, D, 0.0, 1.0, 1.0)
    return values.astype(jnp.bfloat16)


def draw_query_queries(key, part):
    key = jax.random.fold_in(key, 23)
    values = spread_rows(key, QTOKENS, D, 0.0, 1.0, 1.0)
    return values.astype(jnp.bfloat16)


def plant(drawn, own_key, least, largest):
    longest = drawn.shape.index(max(drawn.shape))
    spots = []
    for shift in (0, 1):
        where = [jax.random.randint(jax.random.fold_in(own_key, axis), (), 0, length) for axis, length in enumerate(drawn.shape)]
        where[longest] = (where[longest] + shift) % drawn.shape[longest]
        spots.append(tuple(where))
    return drawn.at[spots[0]].set(least).at[spots[1]].set(largest)


def levels(key, dims, cuts, low, top_value):
    gain = 1.0
    for axis_at, parts in cuts:
        steps = jax.random.uniform(jax.random.fold_in(jax.random.fold_in(key, 6), axis_at), (parts,), jnp.float32, low / len(cuts), top_value / len(cuts))
        gain = gain * jnp.repeat(jnp.exp(steps), dims[axis_at] // parts).reshape((-1,) + (1,) * (len(dims) - 1 - axis_at))
    return gain


def noise(stream_key, shape, spread, most, split=(), kind=jnp.bfloat16):
    drawn = spread * jax.random.normal(stream_key, shape, jnp.float32)
    if split:
        drawn = drawn * levels(stream_key, shape, split, -0.22, 0.18)
    return jnp.clip(drawn, -most, most).astype(kind)


def setup_inputs(seed: int = 0) -> dict:
    arg_keys = jax.random.split(jax.random.key(seed), 16)
    return {
        "summary_states": noise(arg_keys[0], (NSUM, D), 1.0, 6.0, ((0, 64), (1, 4))),
        "summary_queries": draw_summary_queries(jax.random.fold_in(arg_keys[15], 71), 0),
        "summary_keys": noise(arg_keys[2], (NSUM, D), 1.0, 6.0, ((0, 64), (1, 4))),
        "summary_values": noise(arg_keys[3], (NSUM, D), 1.0, 6.0, ((0, 64), (1, 4))),
        "demo_keys": noise(arg_keys[4], (DEMOS, CACHE, D), 1.0, 6.0, ((0, 64), (2, 4))),
        "demo_values": noise(arg_keys[5], (DEMOS, CACHE, D), 1.0, 6.0, ((0, 64), (2, 4))),
        "demo_lengths": plant(jax.random.randint(arg_keys[6], (DEMOS,), CACHE // 4, CACHE + 1), jax.random.fold_in(arg_keys[6], 1), CACHE // 4, CACHE).astype(jnp.int32),
        "out_weight": noise(arg_keys[7], (D, D), D ** -0.5, 0.09375, ((0, 4), (1, 64))),
        "norm_gain": jnp.clip(1.0 + 0.1 * jax.random.normal(arg_keys[8], (D,), jnp.float32), 0.5, 1.5),
        "key_weight": noise(arg_keys[9], (D, D), D ** -0.5, 0.09375, ((0, 64), (1, 4))),
        "value_weight": noise(arg_keys[10], (D, D), D ** -0.5, 0.09375, ((0, 64), (1, 4))),
        "query_queries": draw_query_queries(jax.random.fold_in(arg_keys[15], 71), 0),
        "query_keys": noise(arg_keys[12], (QTOKENS, D), 1.0, 6.0, ((0, 64), (1, 4))),
        "query_values": noise(arg_keys[13], (QTOKENS, D), 1.0, 6.0, ((0, 64), (1, 4))),
        "query_offsets": plant(jax.random.randint(arg_keys[14], (QTOKENS // QLEN,), 0, DEMOS + 1), jax.random.fold_in(arg_keys[14], 1), 0, DEMOS).astype(jnp.int32),
    }


NEG = -1e+30
EPS = 1e-05

def reference(summary_states, summary_queries, summary_keys, summary_values, demo_keys, demo_values, demo_lengths, out_weight, norm_gain, key_weight, value_weight, query_queries, query_keys, query_values, query_offsets):
    scale = HD ** (-0.5)
    f32 = jnp.float32
    qs = summary_queries.reshape(DEMOS, SLOTS, H, HD).astype(f32)
    ks = summary_keys.reshape(DEMOS, SLOTS, H, HD).astype(f32)
    vs = summary_values.reshape(DEMOS, SLOTS, H, HD).astype(f32)
    kc = demo_keys.reshape(DEMOS, CACHE, H, HD).astype(f32)
    vc = demo_values.reshape(DEMOS, CACHE, H, HD).astype(f32)
    cache_scores = jnp.einsum('dshe,dlhe->dhsl', qs, kc) * scale
    own_scores = jnp.einsum('dshe,dthe->dhst', qs, ks) * scale
    cache_mask = (jnp.arange(CACHE)[None, :] < demo_lengths[:, None])[:, None, None, :]
    own_mask = jnp.tril(jnp.ones((SLOTS, SLOTS), bool))[None, None]
    top = jnp.maximum(lax.optimization_barrier(jnp.max(jnp.where(cache_mask, cache_scores, NEG), -1)), lax.optimization_barrier(jnp.max(jnp.where(own_mask, own_scores, NEG), -1)))
    w_cache = jnp.where(cache_mask, jnp.exp(cache_scores - top[..., None]), 0.0)
    w_own = jnp.where(own_mask, jnp.exp(own_scores - top[..., None]), 0.0)
    numer = jnp.einsum('dhsl,dlhe->dshe', w_cache.astype(jnp.bfloat16).astype(f32), vc)
    numer = numer + jnp.einsum('dhst,dthe->dshe', w_own.astype(jnp.bfloat16).astype(f32), vs)
    denom = (lax.optimization_barrier(jnp.sum(w_cache, -1)) + lax.optimization_barrier(jnp.sum(w_own, -1))).transpose(0, 2, 1)[..., None]
    compressed = (numer / denom).astype(jnp.bfloat16).reshape(NSUM, D)
    mixed = summary_states.astype(f32) + jnp.dot(compressed, out_weight, preferred_element_type=f32)
    normed = (mixed * lax.rsqrt(lax.optimization_barrier(jnp.mean(mixed * mixed, axis=1, keepdims=True)) + EPS) * norm_gain[None, :]).astype(jnp.bfloat16)
    compact_keys = jnp.dot(normed, key_weight, preferred_element_type=f32).astype(jnp.bfloat16)
    compact_values = jnp.dot(normed, value_weight, preferred_element_type=f32).astype(jnp.bfloat16)
    examples = QTOKENS // QLEN
    reach = jnp.repeat(query_offsets, QLEN)
    allowed = (jnp.arange(NSUM) // SLOTS)[None, :] < reach[:, None]
    causal = jnp.tril(jnp.ones((QLEN, QLEN), bool))[None]

    def per_head(items):
        qh, kh, vh, skh, svh = items
        far = jnp.dot(qh, skh.T, preferred_element_type=f32) * scale
        qe = qh.reshape(examples, QLEN, HD).astype(f32)
        ke = kh.reshape(examples, QLEN, HD).astype(f32)
        ve = vh.reshape(examples, QLEN, HD).astype(f32)
        near = jnp.einsum('exd,eyd->exy', qe, ke) * scale
        top_far = lax.optimization_barrier(jnp.max(jnp.where(allowed, far, NEG), -1))
        top_near = lax.optimization_barrier(jnp.max(jnp.where(causal, near, NEG), -1)).reshape(QTOKENS)
        best = jnp.maximum(top_far, top_near)
        w_far = jnp.where(allowed, jnp.exp(far - best[:, None]), 0.0)
        w_near = jnp.where(causal, jnp.exp(near - best.reshape(examples, QLEN)[..., None]), 0.0)
        numer = jnp.dot(w_far.astype(jnp.bfloat16), svh, preferred_element_type=f32)
        numer = numer + jnp.einsum('exy,eyd->exd', w_near.astype(jnp.bfloat16).astype(f32), ve).reshape(QTOKENS, HD)
        denom = lax.optimization_barrier(jnp.sum(w_far, -1)) + lax.optimization_barrier(jnp.sum(w_near, -1)).reshape(QTOKENS)
        return (numer / denom[:, None]).astype(jnp.bfloat16)

    def heads_first(array, rows):
        return array.reshape(rows, H, HD).transpose(1, 0, 2)
    outputs = lax.map(per_head, (heads_first(query_queries, QTOKENS), heads_first(query_keys, QTOKENS), heads_first(query_values, QTOKENS), heads_first(compact_keys, NSUM), heads_first(compact_values, NSUM)))
    return outputs.transpose(1, 0, 2).reshape(QTOKENS, D)
```

```python
import functools
import math

import jax
import jax.numpy as jnp
from jax import lax
from jax.experimental import pallas as pl
from jax.experimental.pallas import tpu as pltpu
from jax.sharding import PartitionSpec as P

D = 4096
HD = 128
SLOTS = 8
QLEN = 128
HEADS = 8
WIDTH = HEADS * HD
HALF = WIDTH // 2
NEG = -1e30
EPS = 1e-05
EXPO = HD ** (-0.5) * math.log2(math.e)

f32 = jnp.float32
bf16 = jnp.bfloat16
VM = pl.BlockSpec(memory_space=pltpu.VMEM)
SM = pl.BlockSpec(memory_space=pltpu.SMEM)
ANY = pl.BlockSpec(memory_space=pl.ANY)
NT = (((1,), (1,)), ((), ()))
TN = (((0,), (0,)), ((), ()))
NN = (((1,), (0,)), ((), ()))


SMALL = pl.CostEstimate(flops=1000, bytes_accessed=1000, transcendentals=0)
LARGE = pl.CostEstimate(flops=int(5e10), bytes_accessed=1000, transcendentals=0)


def dot(a, b, dims=NN):
    return lax.dot_general(a, b, dims, preferred_element_type=f32)


def shape(dims, dtype=bf16):
    return jax.ShapeDtypeStruct(dims, dtype)


def call(kernel, outs, n_in, scratch=(), mb=24):
    return pl.pallas_call(
        kernel,
        out_shape=outs,
        in_specs=[SM] + [VM] * n_in,
        out_specs=jax.tree.map(lambda _: VM, outs),
        scratch_shapes=list(scratch),
        cost_estimate=SMALL,
        compiler_params=pltpu.CompilerParams(vmem_limit_bytes=mb << 20),
    )


def after(v, *others):
    return lax.optimization_barrier((v, *others))[0]


def places():
    return [(i >> 4, (i >> 2) & 3, (i >> 1) & 1, i & 1) for i in range(64)]


def index(x, y, z, c):
    return (((x & 3) * 4 + (y & 3)) * 2 + z) * 2 + c


def send(v, to):
    return lax.ppermute(v, "shot", [(i, index(*to(*p))) for i, p in enumerate(places())])


def send_x(v, k):
    return send(v, lambda x, y, z, c: (x + k, y, z, c))


def send_y(v, k):
    return send(v, lambda x, y, z, c: (x, y + k, z, c))


def send_z(v):
    return send(v, lambda x, y, z, c: (x, y, 1 - z, c))


def send_core(v):
    return send(v, lambda x, y, z, c: (x, y, z, 1 - c))


def turn(c, back):
    return (1 - 2 * c) * (-1 if back else 1)


def ring(v, move):
    first = send(v, lambda x, y, z, c: move(x, y, z, c, turn(c, False)))
    second = send(v, lambda x, y, z, c: move(x, y, z, c, turn(c, True)))
    return first, second, lambda u: send(u, lambda x, y, z, c: move(x, y, z, c, turn(c, False)))


def ring_y(v):
    return ring(v, lambda x, y, z, c, k: (x, y + k, z, c))


def ring_head(v):
    def step(u, back):
        pairs = [(i * 4 + h, i * 4 + (h + turn(i & 1, back)) % 4) for i in range(64) for h in range(4)]
        return lax.ppermute(u, ("shot", "head"), pairs)

    first = step(v, False)
    return [first, step(v, True), step(first, False)]


def write_aside(at_ref, states_ref, gain_ref, keep_ref, give_ref, rows_ref):
    y, z, core = at_ref[1], at_ref[2], at_ref[3]
    low = lax.broadcasted_iota(jnp.int32, (16, HD), 1) < HD // 2
    row = lax.broadcasted_iota(jnp.int32, (16, HD), 0)

    def pick(ref, at_z):
        def block(step):
            start = ((y + step) & 3) * 256 + at_z * HD
            return jnp.broadcast_to(ref[:, pl.ds(pl.multiple_of(start, HD), HD)].astype(f32), (16, HD))

        here, back, ahead, over = block(0), block(-1), block(1), block(2)

        def lows(a, b):
            return jnp.where(low, a, pltpu.roll(b, HD // 2, 1))

        def highs(a, b):
            return jnp.where(low, pltpu.roll(a, HD // 2, 1), b)

        zero = [lows(here, back), lows(ahead, over)]
        one = [highs(here, ahead), highs(back, over)]
        return [jnp.where(core == 0, a, b) for a, b in zip(zero + one, one + zero)]

    for k, v in enumerate(pick(states_ref, z)):
        keep_ref[:, WIDTH + k * HD : WIDTH + (k + 1) * HD] = v.astype(bf16)
    for k, v in enumerate(pick(states_ref, 1 - z)):
        give_ref[:, WIDTH + k * HD : WIDTH + (k + 1) * HD] = v.astype(bf16)
    for k, gain in enumerate(pick(gain_ref, z)):
        high = gain.astype(bf16).astype(f32)
        both = jnp.where(row == 0, high, jnp.where(row == 1, gain - high, 0.0))
        rows_ref[:, k * HD : (k + 1) * HD] = both.astype(bf16)


def demo_kernel(
    len_ref, at_ref, q_ref, ks_ref, vs_ref, kc_ref, vc_ref, states_ref, gain_ref, keep_ref, give_ref, rows_ref, total
):
    d = pl.program_id(0)

    @pl.when(d == 0)
    def _():
        write_aside(at_ref, states_ref, gain_ref, keep_ref, give_ref, rows_ref)

    q = q_ref[...].astype(f32)
    mine = jnp.where(d == 0, q[:SLOTS], q[SLOTS:])
    rows = lax.broadcasted_iota(jnp.int32, (HEADS * SLOTS, WIDTH), 0) // SLOTS
    cols = lax.broadcasted_iota(jnp.int32, (HEADS * SLOTS, WIDTH), 1) // HD
    same = rows == cols
    qe = jnp.where(same, jnp.concatenate([mine] * HEADS, axis=0), 0.0).astype(bf16)
    kc = kc_ref[0]
    s = dot(kc, qe, NT)
    so = dot(ks_ref[...], qe, NT)
    at = lax.broadcasted_iota(jnp.int32, s.shape, 0)
    s = jnp.where(at < len_ref[d], s, NEG)
    t = lax.broadcasted_iota(jnp.int32, so.shape, 0)
    slot = lax.broadcasted_iota(jnp.int32, so.shape, 1) % SLOTS
    so = jnp.where((t // SLOTS == d) & (t % SLOTS <= slot), so, NEG)
    top = jnp.maximum(jnp.max(s, 0, keepdims=True), jnp.max(so, 0, keepdims=True))
    p = jnp.exp2((s - top) * EXPO).astype(bf16)
    po = jnp.exp2((so - top) * EXPO).astype(bf16)
    num = dot(p, vc_ref[0], TN) + dot(po, vs_ref[...], TN)
    den = dot(p, jnp.ones((p.shape[0], HD), bf16), TN) + dot(po, jnp.ones((po.shape[0], HD), bf16), TN)
    res = jnp.where(same, num / jnp.concatenate([den] * HEADS, axis=1), 0.0)
    total[pl.ds(pl.multiple_of(d * SLOTS, SLOTS), SLOTS), :] = jnp.sum(res.reshape(HEADS, SLOTS, WIDTH), axis=0)

    @pl.when(d == pl.num_programs(0) - 1)
    def _():
        keep_ref[:, :WIDTH] = total[...].astype(bf16)
        give_ref[:, :WIDTH] = total[...].astype(bf16)


def demo_attention(lengths, at, q, ks, vs, kc, vc, states, gain):
    n, length, _ = kc.shape
    rows = q.shape[0]
    whole = pl.BlockSpec((rows, WIDTH), lambda i, *_: (0, 0))
    cached = pl.BlockSpec((1, length, WIDTH), lambda i, *_: (i, 0, 0))
    return pl.pallas_call(
        demo_kernel,
        out_shape=(shape((rows, WIDTH + HALF)), shape((rows, WIDTH + HALF)), shape((rows, HALF))),
        grid_spec=pltpu.PrefetchScalarGridSpec(
            num_scalar_prefetch=2,
            grid=(n,),
            in_specs=[whole, whole, whole, cached, cached, whole, pl.BlockSpec((1, WIDTH), lambda i, *_: (0, 0))],
            out_specs=[
                pl.BlockSpec((rows, WIDTH + HALF), lambda i, *_: (0, 0)),
                pl.BlockSpec((rows, WIDTH + HALF), lambda i, *_: (0, 0)),
                pl.BlockSpec((rows, HALF), lambda i, *_: (0, 0)),
            ],
            scratch_shapes=[pltpu.VMEM((rows, WIDTH), f32)],
        ),
        cost_estimate=SMALL,
        compiler_params=pltpu.CompilerParams(vmem_limit_bytes=60 << 20),
    )(lengths, at, q, ks, vs, kc, vc, states, gain.reshape(1, WIDTH))


def eye(n):
    row = lax.broadcasted_iota(jnp.int32, (n, n), 0)
    col = lax.broadcasted_iota(jnp.int32, (n, n), 1)
    return (row == col).astype(f32).astype(bf16)


def near_kernel(group, at_ref, q_ref, k_ref, v_ref, *refs):
    row = lax.broadcasted_iota(jnp.int32, (QLEN, QLEN), 0)
    col = lax.broadcasted_iota(jnp.int32, (QLEN, QLEN), 1)
    causal = row <= col
    o_ref, l_ref = refs[-2:]
    cuts = [slice(j * HD, (j + 1) * HD) for j in range(HEADS)]
    for e in range(group):
        to = slice(e * QLEN, (e + 1) * QLEN)
        scores = [jnp.where(causal, dot(k_ref[to, at], q_ref[to, at], NT), NEG) for at in cuts]
        tops = [jnp.max(s, 0, keepdims=True) * EXPO for s in scores]
        weights = [jnp.exp2(s * EXPO - top) for s, top in zip(scores, tops)]
        dens = [jnp.sum(p, 0, keepdims=True) for p in weights]
        sums = [dot(v_ref[to, at], p.astype(bf16), TN) for p, at in zip(weights, cuts)]
        for j, at in enumerate(cuts):
            o_ref[0, at, to] = (sums[j] * (1.0 / dens[j])).astype(bf16)
            l_ref[0, j : j + 1, to] = tops[j] + jnp.log2(dens[j])


def state_shapes(q, group):
    return shape((q.shape[0] // (group * QLEN), WIDTH, group * QLEN)), shape(
        (q.shape[0] // (group * QLEN), HEADS, group * QLEN), f32
    )


def state_specs(group):
    return [
        pl.BlockSpec((1, WIDTH, group * QLEN), lambda g: (g, 0, 0)),
        pl.BlockSpec((1, HEADS, group * QLEN), lambda g: (g, 0, 0)),
    ]


def query_spec(group):
    return pl.BlockSpec((group * QLEN, WIDTH), lambda g: (g, 0))


def near_attention(at, q, k, v, begin, count, state=(), group=2):
    block = pl.BlockSpec((group * QLEN, WIDTH), lambda g: (g + begin, 0))
    return pl.pallas_call(
        functools.partial(near_kernel, group),
        out_shape=state_shapes(q, group),
        grid=(count,),
        in_specs=[SM] + [block] * 3 + [ANY] * len(state),
        out_specs=[
            pl.BlockSpec((1, WIDTH, group * QLEN), lambda g: (g + begin, 0, 0)),
            pl.BlockSpec((1, HEADS, group * QLEN), lambda g: (g + begin, 0, 0)),
        ],
        input_output_aliases={4 + i: i for i in range(len(state))},
        cost_estimate=LARGE,
        compiler_params=pltpu.CompilerParams(vmem_limit_bytes=58 << 20),
    )(at, q, k, v, *state)


def out_kernel(at_ref, *refs):
    c, w, (g_ref, own_ref, give_ref) = refs[:4], refs[4:12], refs[12:]
    mine = (at_ref[4] == at_ref[0]).astype(f32)
    rows = jnp.concatenate([r[:, :WIDTH] for r in c], axis=0)
    cols = jnp.concatenate([r[...] for r in w], axis=0)
    states = jnp.concatenate([r[:, WIDTH:] for r in c], axis=0).astype(f32)
    total = dot(rows, cols, NT) + states * mine
    gain = g_ref[...].astype(f32) * mine
    own_ref[:128, :] = total
    own_ref[128:, :] = gain
    give_ref[:128, :] = total.astype(bf16)
    give_ref[128:, :] = gain.astype(bf16)


def spread(power):
    lane = lax.broadcasted_iota(jnp.int32, (power.shape[0], HD), 1)
    high = power.astype(bf16).astype(f32)
    return jnp.where(lane == 0, high, jnp.where(lane == 1, power - high, 0.0)).astype(bf16)


WIDE = 2 * WIDTH + HD


def project_kernel(at_ref, own_ref, a_ref, b_ref, c_ref, *refs):
    w, outs = refs[:8], refs[8:]
    total = own_ref[...] + a_ref[...].astype(f32) + b_ref[...].astype(f32) + c_ref[...].astype(f32)
    gain = total[128:129, :] + total[129:130, :]
    mixed = total[:128, :]
    power = jnp.sum(mixed * mixed, axis=1, keepdims=True)
    y = (mixed * gain).astype(bf16)
    lane = lax.broadcasted_iota(jnp.int32, (32, HD), 1)
    for side in range(2):
        to = slice(side * WIDTH, (side + 1) * WIDTH)
        res = dot(y, jnp.concatenate([r[64 * side : 64 * side + 64, :] for r in w], axis=0))
        for k, r in enumerate(outs):
            r[:, to] = res[k * 32 : (k + 1) * 32, :].astype(r.dtype)
    for k, r in enumerate(outs):
        part = power[k * 32 : (k + 1) * 32, :]
        r[:, 2 * WIDTH :] = jnp.where(lane == 0, part, 0.0) if k == 0 else spread(part)


def half_kernel(at_ref, own_ref, a_ref, b_ref, c_ref, keep_ref, give_ref):
    total = own_ref[...] + a_ref[...].astype(f32) + b_ref[...].astype(f32) + c_ref[...].astype(f32)
    keep_ref[...] = total
    give_ref[:, : 2 * WIDTH] = total[:, : 2 * WIDTH].astype(bf16)
    give_ref[:, 2 * WIDTH :] = spread(jnp.sum(total[:, 2 * WIDTH :], axis=1, keepdims=True))


def compact_kernel(at_ref, own_ref, a_ref, keep_ref, give_ref):
    core = at_ref[3]
    total = own_ref[...] + a_ref[...].astype(f32)
    power = jnp.sum(total[:, 2 * WIDTH :], axis=1, keepdims=True)
    factor = lax.rsqrt(power / D + EPS)
    keys, values = total[:, :WIDTH] * factor, total[:, WIDTH : 2 * WIDTH] * factor
    keep_ref[...] = jnp.where(core == 0, keys, values).astype(bf16)
    give_ref[...] = jnp.where(core == 0, values, keys).astype(bf16)


STEP = (0, -1, 1, 2)


def far_kernel(chunks, last, group, ahead, at_ref, off_ref, q_ref, o_ref, l_ref, own_ref, recv_ref, *refs):
    n = len(chunks)
    if last:
        out_ref, keys, turned, values, mask, sems = refs
    else:
        out_ref, newl_ref, keys, turned, values, mask, sems = refs
    g = pl.program_id(0)
    core = at_ref[3]
    rows = 256
    swap = {1: 2, 2: 1}
    cuts = [slice(j * HD, (j + 1) * HD) for j in range(HEADS)]

    def fetch(k_ref, v_ref):
        copies = [pltpu.make_async_copy(k_ref, keys, sems.at[n])]
        for i, t in enumerate(chunks):
            j = chunks.index(swap.get(t, t))
            copies.append(
                pltpu.make_async_copy(
                    v_ref.at[pl.ds(j * rows, rows), :], turned.at[pl.ds(i * rows, rows), :], sems.at[i]
                )
            )
        for copy in copies:
            copy.start()
        for copy in copies:
            copy.wait()

    @pl.when((g == 0) & (core == 0))
    def _():
        fetch(own_ref, recv_ref)

    @pl.when((g == 0) & (core == 1))
    def _():
        fetch(recv_ref, own_ref)

    @pl.when(g == 0)
    def _():
        same = eye(HD)
        for i in range(n):
            to = slice(i * rows, (i + 1) * rows)
            for h in range(HEADS):
                values[h, :HD, to] = dot(same, turned[to, cuts[h]], NT).astype(bf16)
        values[:, HD:, :] = jnp.ones((HEADS, 16, n * rows), bf16)
        x, y = at_ref[0], at_ref[1]
        lane = lax.broadcasted_iota(jnp.int32, (rows, HD), 1)
        offsets = jnp.zeros((rows, HD), jnp.int32)
        for e in range(8):
            offsets = jnp.where(lane == e, off_ref[e], offsets)
        r = lax.broadcasted_iota(jnp.int32, (rows, HD), 0)
        part, inside = r // 64, ((r // 16) % 2) * 4 + ((r // 32) % 2) * 2 + (r % 16) // SLOTS
        for i, t in enumerate(chunks):
            demo = (((x - part) & 3) * 4 + ((y + STEP[t]) & 3)) * 8 + inside
            mask[i * rows : (i + 1) * rows, :] = jnp.where(demo < offsets, 0.0, NEG).astype(bf16)

    lane = lax.broadcasted_iota(jnp.int32, (group * QLEN, HD), 1)
    row = lax.broadcasted_iota(jnp.int32, (group * QLEN, HD), 0)
    which = (lane == group * g + row // QLEN).astype(f32).astype(bf16)

    def score(j):
        k = jnp.concatenate([keys[:, cuts[j]], mask[...]], axis=1)
        return dot(k, jnp.concatenate([q_ref[:, cuts[j]], which], axis=1), NT)

    def weigh(j, s):
        before = l_ref[0, j : j + 1, :]
        top = jnp.maximum(jnp.max(s, 0, keepdims=True) * EXPO, before)
        return top, jnp.exp2(before - top), jnp.exp2(s * EXPO - top).astype(bf16)

    def finish(j, top, w, p):
        r = dot(values[j], p)
        den = r[HD : HD + 1, :] + w
        res = (o_ref[0, cuts[j], :].astype(f32) * w + r[:HD, :]) * (1.0 / den)
        if last:
            out_ref[:, cuts[j]] = jnp.transpose(res).astype(bf16)
        else:
            out_ref[0, cuts[j], :] = res.astype(bf16)
            newl_ref[0, j : j + 1, :] = top + jnp.log2(den)

    scores = [score(j) for j in range(ahead)]
    ready = []
    for j in range(HEADS):
        if j + ahead < HEADS:
            scores.append(score(j + ahead))
        ready.append(weigh(j, scores[j]))
        if j >= ahead:
            finish(j - ahead, *ready[j - ahead])
    for j in range(HEADS - ahead, HEADS):
        finish(j, *ready[j])


def far_attention(at, offsets, q, state, own, recv, chunks, last, group=2, ahead=1):
    n = len(chunks)
    outs, specs = (shape(q.shape), query_spec(group)) if last else (state_shapes(q, group), state_specs(group))
    return pl.pallas_call(
        functools.partial(far_kernel, chunks, last, group, ahead),
        out_shape=outs,
        grid=(q.shape[0] // (group * QLEN),),
        in_specs=[SM, SM, query_spec(group), *state_specs(group), ANY, ANY],
        out_specs=specs,
        scratch_shapes=[
            pltpu.VMEM((n * 256, WIDTH), bf16),
            pltpu.VMEM((n * 256, WIDTH), bf16),
            pltpu.VMEM((HEADS, HD + 16, n * 256), bf16),
            pltpu.VMEM((n * 256, HD), bf16),
            pltpu.SemaphoreType.DMA((n + 1,)),
        ],
        cost_estimate=LARGE,
        compiler_params=pltpu.CompilerParams(vmem_limit_bytes=24 << 20),
    )(at, offsets, q, *state, own, recv)


def per_device(
    summary_states,
    summary_queries,
    summary_keys,
    summary_values,
    demo_keys,
    demo_values,
    demo_lengths,
    out_weight,
    norm_gain,
    key_weight,
    value_weight,
    query_queries,
    query_keys,
    query_values,
    query_offsets,
):
    shot = lax.axis_index("shot")
    head = lax.axis_index("head")
    x, y, z, c = shot >> 4, (shot >> 2) & 3, (shot >> 1) & 1, shot & 1
    at = jnp.stack([x, y, z, c, head]).astype(jnp.int32)
    core0 = c == 0

    out_t = out_weight.T
    out1, out2, pass_out = ring_y(out_t)
    kv = jnp.concatenate([key_weight, value_weight], axis=0)

    mine, give, gain_rows = demo_attention(
        demo_lengths, at, summary_queries, summary_keys, summary_values, demo_keys, demo_values, summary_states, norm_gain
    )
    theirs = send_z(after(give, out1, out2))
    out_parts = [out_t, out1, out2, pass_out(after(out1, give))]
    out_parts += [send_core(after(v, give)) for v in out_parts]
    pair = jnp.where(z == 0, jnp.concatenate([mine, theirs], axis=0), jnp.concatenate([theirs, mine], axis=0))
    rows = [pair] + [send_x(pair, k) for k in (1, 2, 3)]
    queries = query_queries, query_keys, query_values
    state = near_attention(after(at, pair), *queries, 0, 1)
    rows[0] = after(rows[0], state[1])


    own, give = call(out_kernel, (shape((144, HALF), f32), shape((144, HALF))), 13)(at, *rows, *out_parts, gain_rows)
    got = ring_head(give)
    kv1, kv2, pass_kv = ring_y(after(kv, give))
    kv_parts = [kv, kv1, kv2, pass_kv(after(kv1, got[0], got[1]))]
    kv_parts += [send_core(after(v, got[0], got[1])) for v in kv_parts[:3]] + [send_core(after(kv_parts[3], got[2]))]

    parts = call(project_kernel, (shape((32, WIDE), f32),) + (shape((32, WIDE)),) * 3, 12)(at, own, *got, *kv_parts)
    got = [send_x(parts[k], -k) for k in (1, 2, 3)]
    keep, give = call(half_kernel, (shape((32, WIDE), f32), shape((32, WIDE))), 4)(at, parts[0], *got)
    keep, give = call(compact_kernel, (shape((32, WIDTH)),) * 2, 2)(at, keep, send_z(give))
    got = send_core(give)

    row = jnp.where(core0, jnp.concatenate([keep, got], axis=0), jnp.concatenate([got, keep], axis=0))
    others = [send_x(row, k) for k in (1, 2, 3)]
    state = near_attention(after(at, row), *queries, 1, 3, state)
    plane = jnp.concatenate([after(row, state[1])] + others, axis=0)
    plane1, plane2, pass_plane = ring_y(plane)

    def far(state, chunks, *own):
        own = jnp.concatenate(own, axis=0)
        return far_attention(at, query_offsets, query_queries, state, own, send_core(own), chunks, chunks[-1] == 3)

    state = far(state, (0,), plane)
    plane3 = pass_plane(after(plane1, state[1]))
    state = far(state, (1, 2), after(plane1, state[1]), plane2)
    return far(state, (3,), after(plane3, state[1]))


def solution(mesh):
    return jax.shard_map(
        per_device,
        mesh=mesh,
        in_specs=(
            P("shot", "head"),
            P("shot", "head"),
            P("shot", "head"),
            P("shot", "head"),
            P("shot", None, "head"),
            P("shot", None, "head"),
            P("shot"),
            P("head", "shot"),
            P("head"),
            P("shot", "head"),
            P("shot", "head"),
            P("shot", "head"),
            P("shot", "head"),
            P("shot", "head"),
            P("shot"),
        ),
        out_specs=P("shot", "head"),
        check_vma=False,
    )
```
